32 devices in a mesh: grp: 2 (over x), ad: 8 (over z, y), tp: 2 (over core).
Axes of the slice: x: 2, y: 2, z: 4, core: 2. Of those that a mesh axis runs over, the one named last changes fastest.
Arguments:
- tokens: bfloat16 [2048, 8192], P(('grp', 'ad'), 'tp'), parts along dimension 0, may hold values from -6 to 6
- row_adapter_index: int32 [2048, 1], P(('grp', 'ad')), parts along dimension 0, may hold values from 0 to 7; in each aligned block of 128 rows (0 to 127, 128 to 255, ...) at most 32 rows name the same one
- key_base_matrix: bfloat16 [8192, 1024], P('tp'), may hold values from -0.0625 to 0.0625
- adapter_down_factor: bfloat16 [16, 8192, 64], P(('grp', 'ad'), 'tp'), parts along dimension 0, may hold values from -0.0625 to 0.0625
- adapter_up_factor: bfloat16 [16, 64, 1024], P(('grp', 'ad'), None, 'tp'), parts along dimension 0, may hold values from -0.75 to 0.75
Outputs:
- keys: bfloat16 [2048, 1024], P(('grp', 'ad'), 'tp'), parts along dimension 0
The draws below stay inside these ranges and needn't reach their ends.
There are 2 independent parts, one for each index of `grp`. The reference program is written for one: setup_inputs(seed, part) draws one part's arguments, and reference() takes and returns one part's arrays. A program takes and returns all parts, laid end to end along the dimension named above; an argument that names none is the same for every part. Nothing has to cross between parts.
Inputs may be any that keep to these rules, and one draw needn't show every extreme that they name: `row_adapter_index`: among the rows of one index of ad, at most 32 name the same adapter, and in every draw some adapter is named exactly 32 times by the rows of some index.
All inputs are finite; a program needn't handle non-finite values.
Results may differ from the reference program's by a relative error of at most 0.005.
Values may be sent and summed in bfloat16 or wider, within the bound.
A program may use at most 64 MiB of HBM per device.

```python
import math
import jax
import jax.numpy as jnp
import numpy as np
from jax import lax

MODEL_WIDTH = 8192
KEY_FEATURES = 1024
ADAPTER_RANK = 64
ROWS_DEV = 128
ROWS = 1024
ADAPTER_COUNT = 8
CAP = 32


def level_of(own_key, shape, shards, smallest, largest):
    factor_of, own = 1.0, jax.random.fold_in(own_key, 6)
    for dim, blocks in shards:
        steps = jnp.exp(jax.random.uniform(jax.random.fold_in(own, dim), (blocks,), jnp.float32, smallest / len(shards), largest / len(shards)))
        factor_of = factor_of * jnp.repeat(steps, shape[dim] // blocks).reshape([-1 if axis == dim else 1 for axis in range(len(shape))])
    return factor_of


def assign_block(stream_key, own, number, rows, count, top, bound, skew):
    order = jax.random.permutation(stream_key, count)
    heavy_load, ordinary = shares(count, rows * top, bound, skew, True), shares(count, rows * top, bound, skew, False)
    places = jnp.arange(count)

    def named(tallies, rotation):
        used = int((tallies > 0).sum())
        fixed = max(1, used // 4)
        passed = fixed + (places - fixed + rotation * (used - fixed)) % max(1, count - fixed)
        return jnp.zeros((count,), jnp.int32).at[order[jnp.where(places < fixed, places, passed)]].set(jnp.asarray(tallies, jnp.int32))

    tallies = jnp.where(number % 4 == 0, named(heavy_load, number // 4), named(ordinary, number - number // 4 - 1))
    mixed = jax.random.permutation(jax.random.fold_in(own, 3), count)
    source_of, receiver = mixed[0:count // 2 * 2:2], mixed[1:count // 2 * 2:2]
    margin = jnp.minimum(tallies[source_of] - 1, bound - tallies[receiver]) // 2
    margin = jnp.where((source_of == order[0]) | (receiver == order[0]) | (tallies[receiver] == 0), 0, jnp.maximum(margin, 0))
    passed = jax.random.randint(jax.random.fold_in(own, 4), (count // 2,), 0, 1 << 20) % (margin + 1)
    tallies = tallies.at[source_of].add(-passed).at[receiver].add(passed)
    items = jnp.searchsorted(jnp.cumsum(tallies), jnp.arange(rows * top), side="right").astype(jnp.int32)
    listing = items.reshape(top, rows).T
    listing = listing[jax.random.permutation(jax.random.fold_in(own, 1), rows)]
    rotation = jax.random.randint(jax.random.fold_in(own, 2), (rows, 1), 0, top)
    return jnp.take_along_axis(listing, (jnp.arange(top)[None, :] + rotation) % top, axis=1)


def shares(count, total, reach, slope, full):
    weights = [(1 << 20) // math.isqrt(standing ** slope) + 1 for standing in range(1, count + 1)]
    largest = reach if full else min(reach, max(-(-total // count), total * weights[0] // sum(weights)))
    least = 1 if total - largest >= count - 1 else 0
    counts, rest = [largest] + [least] * (count - 1), total - largest - least * (count - 1)
    while rest > 0:
        free = [i for i in range(1, count) if counts[i] < largest] or [i for i in range(1, count) if counts[i] < reach]
        whole, left = sum([weights[i] for i in free]), rest
        for i in free:
            extra = min(reach - counts[i], max(1, left * weights[i] // whole), rest)
            counts[i] = counts[i] + extra
            rest = rest - extra
    return np.array(counts)


def scatter_about(own_key, shape, spread, bound, split=(), dtype=jnp.bfloat16):
    level = level_of(own_key, shape, split, -0.22, 0.18) if split else 1.0
    drawn = jax.random.normal(own_key, shape, jnp.float32) * spread * level
    return jnp.minimum(jnp.maximum(drawn, -bound), bound).astype(dtype)


def setup_inputs(seed: int = 0, part: int = 0) -> dict:
    seeds = jax.random.split(jax.random.key(seed), 6)
    part_keys = jax.random.split(jax.random.fold_in(seeds[5], part), 6)
    tokens = scatter_about(part_keys[0], (ROWS, MODEL_WIDTH), 1.0, 6.0, ((0, 8), (1, 2)))
    row_adapter_index_keys = jax.random.split(jax.random.fold_in(part_keys[1], 1), ROWS // ROWS_DEV)
    row_adapter_index_turns = jax.random.permutation(jax.random.fold_in(part_keys[1], 3), ROWS // ROWS_DEV)
    row_adapter_index = jax.vmap(lambda own, number: assign_block(jax.random.fold_in(part_keys[1], 2), own, number, ROWS_DEV, ADAPTER_COUNT, 1, CAP, 2))(row_adapter_index_keys, row_adapter_index_turns).reshape((ROWS, 1))
    key_base_matrix = scatter_about(seeds[2], (MODEL_WIDTH, KEY_FEATURES), MODEL_WIDTH ** -0.5, 0.0625, ((0, 2),))
    adapter_down_factor = scatter_about(part_keys[3], (ADAPTER_COUNT, MODEL_WIDTH, ADAPTER_RANK), MODEL_WIDTH ** -0.5, 0.0625, ((0, 8), (1, 2)))
    adapter_up_factor = scatter_about(part_keys[4], (ADAPTER_COUNT, ADAPTER_RANK, KEY_FEATURES), ADAPTER_RANK ** -0.5, 0.75, ((0, 8), (2, 2)))
    return {"tokens": tokens, "row_adapter_index": row_adapter_index, "key_base_matrix": key_base_matrix, "adapter_down_factor": adapter_down_factor, "adapter_up_factor": adapter_up_factor}


def reference(tokens, row_adapter_index, key_base_matrix, adapter_down_factor, adapter_up_factor):
    projected = jnp.dot(tokens, key_base_matrix, preferred_element_type=jnp.float32)
    row_adapter = row_adapter_index[:, 0].astype(jnp.int32)

    def per_block(pair):
        block_rows, block_index_list = pair
        down_factor_rows = adapter_down_factor[block_index_list].astype(jnp.float32)
        shrunk = jnp.einsum("rd,rdk->rk", block_rows.astype(jnp.float32), down_factor_rows)
        shrunk = lax.optimization_barrier(shrunk.astype(jnp.bfloat16))
        up_factor_rows = adapter_up_factor[block_index_list].astype(jnp.float32)
        expanded = jnp.einsum("rk,rkn->rn", shrunk.astype(jnp.float32), up_factor_rows)
        return expanded.astype(jnp.bfloat16)

    expanded = lax.map(per_block, (tokens.reshape(ROWS // 8, 8, MODEL_WIDTH), row_adapter.reshape(ROWS // 8, 8)))
    expanded = lax.optimization_barrier(expanded.reshape(ROWS, KEY_FEATURES))
    return (projected + expanded.astype(jnp.float32)).astype(jnp.bfloat16)
```

```python
import functools

import jax
import jax.numpy as jnp
from jax import lax
from jax.experimental import pallas as pl
from jax.experimental.pallas import tpu as pltpu
from jax.sharding import PartitionSpec as P

MESH = pl.DeviceIdType.MESH
LANES = 128
BASE_CHUNKS = 8


def flip(index, bits):
    result, bit = index, 1
    while bit <= bits:
        if bits & bit:
            result = result + bit * (1 - 2 * lax.rem(lax.div(index, bit), 2))
        bit *= 2
    return result


def feature_kernel(
    ad_count, group,
    tok, idx, base, down, up, out,
    tok_own, base_all, down_own, packed, gtok, gdown, gup, idx_own, idx_send, gidx,
    ids, acc, part_out, part_in, base_acc, base_in,
    local_sem, chunk_sem, tok_send, tok_recv, down_send, down_recv, up_send, up_recv,
    idx_ssem, idx_rsem, part_send, part_recv, base_send, base_recv,
):
    grp, me, tp = lax.axis_index("grp"), lax.axis_index("ad"), lax.axis_index("tp")
    rows, half_width = tok.shape
    slice_width = half_width // group
    part_width = slice_width // 2
    rank, out_width = up.shape[1], up.shape[2]
    other = 1 - tp
    own_member = lax.rem(me, group)

    def device(slot, cross=0):
        return (grp, flip(me, slot), other if cross else tp)

    def columns(member):
        return pl.ds(pl.multiple_of(member * slice_width, slice_width), slice_width)

    loads = [
        pltpu.make_async_copy(down.at[0], down_own, local_sem.at[0]),
        pltpu.make_async_copy(idx, idx_own, local_sem.at[1]),
        pltpu.make_async_copy(tok, tok_own, local_sem.at[2]),
        pltpu.make_async_copy(tok.at[:, columns(own_member)], gtok.at[0], local_sem.at[3]),
        pltpu.make_async_copy(up.at[0], gup.at[pl.ds(0, rank)], local_sem.at[4]),
    ]
    for load in loads:
        load.start()
    depth = half_width // BASE_CHUNKS
    chunks = [
        pltpu.make_async_copy(
            base.at[pl.ds(c * depth, depth)], base_all.at[pl.ds(c * depth, depth)], chunk_sem.at[c]
        )
        for c in range(BASE_CHUNKS)
    ]
    for chunk in chunks:
        chunk.start()

    barrier = pltpu.get_barrier_semaphore()
    greeted = [(s, 0) for s in range(1, ad_count)] + [(s, 1) for s in range(group)]
    for s, cross in greeted:
        pl.semaphore_signal(barrier, inc=1, device_id=device(s, cross), device_id_type=MESH)
    pl.semaphore_wait(barrier, len(greeted))

    tok_copies = {}
    for s in range(group - 1, 0, -1):
        tok_copies[s] = pltpu.make_async_remote_copy(
            src_ref=tok.at[:, columns(lax.rem(flip(me, s), group))],
            dst_ref=gtok.at[s],
            send_sem=tok_send.at[s], recv_sem=tok_recv.at[s],
            device_id=device(s), device_id_type=MESH,
        )
        tok_copies[s].start()

    loads[0].wait()
    for q in range(group):
        left = down_own[q * slice_width:q * slice_width + part_width, :]
        right = down_own[q * slice_width + part_width:(q + 1) * slice_width, :]
        packed[q] = jnp.concatenate([left, right], axis=1)
    down_copies = {}
    for s in range(ad_count - 1, 0, -1):
        down_copies[s] = pltpu.make_async_remote_copy(
            src_ref=packed.at[lax.rem(flip(me, s), group)],
            dst_ref=gdown.at[:, pl.ds(s * LANES, LANES)],
            send_sem=down_send.at[s], recv_sem=down_recv.at[s],
            device_id=device(s), device_id_type=MESH,
        )
        down_copies[s].start()

    loads[1].wait()
    wide = jnp.broadcast_to(idx_own[...].astype(jnp.float32), (rows, LANES))
    ids[0] = wide.astype(jnp.int32)
    idx_send[...] = wide.T[0:8, :]
    idx_copies = {}
    for s in range(group - 1, 0, -1):
        idx_copies[s] = pltpu.make_async_remote_copy(
            src_ref=idx_send, dst_ref=gidx.at[s],
            send_sem=idx_ssem.at[s], recv_sem=idx_rsem.at[s],
            device_id=device(s), device_id_type=MESH,
        )
        idx_copies[s].start()

    up_copies = {}

    def send_up(source, slot, to):
        up_copies[slot] = pltpu.make_async_remote_copy(
            src_ref=source, dst_ref=gup.at[pl.ds(slot * rank, rank)],
            send_sem=up_send.at[slot], recv_sem=up_recv.at[slot],
            device_id=device(to), device_id_type=MESH,
        )
        up_copies[slot].start()

    for s in list(range(ad_count - 2, 0, -2)) + [1]:
        send_up(up.at[0], s, s)

    gdown[:, 0:LANES] = packed[own_member]

    loads[2].wait()
    base_acc[...] = jnp.zeros_like(base_acc)
    for chunk in chunks:
        chunk.wait()

    @pl.loop(0, BASE_CHUNKS)
    def _(c):
        span = pl.ds(pl.multiple_of(c * depth, depth), depth)
        base_acc[...] += jnp.dot(
            tok_own[:, span], base_all[span, :], preferred_element_type=jnp.float32
        )

    base_copy = pltpu.make_async_remote_copy(
        src_ref=base_acc.at[:, pl.ds(pl.multiple_of(other * out_width, out_width), out_width)],
        dst_ref=base_in,
        send_sem=base_send.at[0], recv_sem=base_recv.at[0],
        device_id=device(0, 1), device_id_type=MESH,
    )
    base_copy.start()

    for s in range(2, ad_count, 2):
        up_copies[s].wait_recv()
        send_up(gup.at[pl.ds(s * rank, rank)], s + 1, 1)

    for s in range(1, group):
        idx_copies[s].wait_recv()
        ids[s] = jnp.broadcast_to(gidx[s][0:1, :], (LANES, rows)).T.astype(jnp.int32)
    loads[3].wait()
    for s in range(1, group):
        tok_copies[s].wait_recv()

    low = lax.broadcasted_iota(jnp.int32, (rows, LANES), 1) < rank
    for p in range(0, ad_count, 2):
        for s in (p, p + 1):
            if s:
                down_copies[s].wait_recv()
        factors = gdown[:, p * LANES:(p + 2) * LANES]
        for m in range(group):
            left = jnp.dot(gtok[m, :, :part_width], factors, preferred_element_type=jnp.float32)
            right = jnp.dot(gtok[m, :, part_width:], factors, preferred_element_type=jnp.float32)
            total = jnp.zeros((rows, LANES), jnp.float32) if p == 0 else acc[m]
            for k in range(2):
                both = jnp.where(
                    low, left[:, k * LANES:(k + 1) * LANES], right[:, k * LANES:(k + 1) * LANES]
                )
                total = jnp.where(ids[m] == flip(me, p + k), both, total)
            acc[m] = total

    part_copies = []
    for m in list(range(group - 1, 0, -1)) + [0]:
        whole = acc[m]
        whole = whole + pltpu.roll(whole, rank, 1)
        part_out[m] = jnp.where(low[:rows // 2], whole[:rows // 2], whole[rows // 2:])
        for cross in (0, 1):
            if m or cross:
                copy = pltpu.make_async_remote_copy(
                    src_ref=part_out.at[m], dst_ref=part_in.at[2 * m + cross],
                    send_sem=part_send.at[2 * m + cross], recv_sem=part_recv.at[2 * m + cross],
                    device_id=device(m, cross), device_id_type=MESH,
                )
                copy.start()
                part_copies.append(copy)

    base_copy.wait_recv()
    kept = base_acc[:, pl.ds(pl.multiple_of(tp * out_width, out_width), out_width)] + base_in[...]
    for s in range(1, ad_count, 2):
        up_copies[s].wait_recv()
    loads[4].wait()

    shrunk = part_out[0]
    for copy in part_copies:
        copy.wait_recv()
    for slot in range(1, 2 * group):
        shrunk = shrunk + part_in[slot]
    turned = pltpu.roll(shrunk, rank, 1)
    low_half = low[:rows // 2]
    spread = jnp.concatenate(
        [jnp.where(low_half, shrunk, turned), jnp.where(low_half, turned, shrunk)], axis=0
    )
    placed = []
    for p in range(0, ad_count, 2):
        named = jnp.where(low, flip(me, p), flip(me, p + 1))
        placed.append(jnp.where(ids[0] == named, spread, 0.0).astype(jnp.bfloat16))
    expanded = jnp.dot(
        jnp.concatenate(placed, axis=1), gup[...], preferred_element_type=jnp.float32
    ).astype(jnp.bfloat16)
    out[...] = (kept + expanded.astype(jnp.float32)).astype(jnp.bfloat16)

    for copies in (tok_copies, down_copies, idx_copies, up_copies):
        for s in copies:
            copies[s].wait_send()
    for copy in part_copies:
        copy.wait_send()
    base_copy.wait_send()


def by_features(ad_count, group, tokens, row_adapter_index, key_base_matrix, down, up):
    rows, half_width = tokens.shape
    key_width = key_base_matrix.shape[1]
    rank, out_width = up.shape[1], up.shape[2]
    slice_width = half_width // group
    bf16, f32, i32 = jnp.bfloat16, jnp.float32, jnp.int32
    dma = pltpu.SemaphoreType.DMA
    return pl.pallas_call(
        functools.partial(feature_kernel, ad_count, group),
        out_shape=jax.ShapeDtypeStruct((rows, out_width), bf16),
        in_specs=[pl.BlockSpec(memory_space=pl.ANY)] * 5,
        out_specs=pl.BlockSpec(memory_space=pltpu.VMEM),
        scratch_shapes=[
            pltpu.VMEM((rows, half_width), bf16),
            pltpu.VMEM((half_width, key_width), bf16),
            pltpu.VMEM((half_width, rank), bf16),
            pltpu.VMEM((group, slice_width // 2, LANES), bf16),
            pltpu.VMEM((group, rows, slice_width), bf16),
            pltpu.VMEM((slice_width // 2, ad_count * LANES), bf16),
            pltpu.VMEM((ad_count * rank, out_width), bf16),
            pltpu.VMEM((rows, 1), i32),
            pltpu.VMEM((8, rows), f32),
            pltpu.VMEM((group, 8, rows), f32),
            pltpu.VMEM((group, rows, LANES), i32),
            pltpu.VMEM((group, rows, LANES), f32),
            pltpu.VMEM((group, rows // 2, LANES), f32),
            pltpu.VMEM((2 * group, rows // 2, LANES), f32),
            pltpu.VMEM((rows, key_width), f32),
            pltpu.VMEM((rows, out_width), f32),
            dma((5,)), dma((BASE_CHUNKS,)),
            dma((group,)), dma((group,)),
            dma((ad_count,)), dma((ad_count,)),
            dma((ad_count,)), dma((ad_count,)),
            dma((group,)), dma((group,)),
            dma((2 * group,)), dma((2 * group,)),
            dma((1,)), dma((1,)),
        ],
        compiler_params=pltpu.CompilerParams(
            collective_id=0, has_side_effects=True, vmem_limit_bytes=48 * 1024 * 1024
        ),
        cost_estimate=pl.CostEstimate(
            flops=2 * rows * half_width * (key_width + 2 * ad_count * rank),
            bytes_accessed=2 * half_width * (key_width + 2 * rows + rank),
            transcendentals=0,
        ),
    )(tokens, row_adapter_index, key_base_matrix, down, up)


def by_rows(ad_count, tokens, row_adapter_index, key_base_matrix, down, up):
    row_count, feature_half = tokens.shape
    capacity = max(2, 2 * row_count // ad_count)
    row_adapter = row_adapter_index[:, 0]
    one_hot = (row_adapter[:, None] == jnp.arange(ad_count, dtype=jnp.int32)[None, :]).astype(
        jnp.int32
    )
    earlier = jnp.cumsum(one_hot, axis=0) - one_hot
    position = row_adapter * capacity + jnp.sum(earlier * one_hot, axis=1)
    outgoing = jnp.zeros((ad_count * capacity, feature_half), jnp.bfloat16).at[position].set(tokens)
    outgoing = outgoing.reshape(ad_count, capacity, feature_half)
    received = lax.all_to_all(outgoing, "ad", split_axis=0, concat_axis=0, tiled=True)
    flat_rows = received.reshape(ad_count * capacity, feature_half)
    shrunk_part = jnp.dot(flat_rows, down[0], preferred_element_type=jnp.float32)
    shrunk = lax.psum(shrunk_part, "tp").astype(jnp.bfloat16)
    expanded = jnp.dot(shrunk, up[0], preferred_element_type=jnp.float32).astype(jnp.bfloat16)
    expanded = expanded.reshape(ad_count, capacity, up.shape[2])
    returned = lax.all_to_all(expanded, "ad", split_axis=0, concat_axis=0, tiled=True)
    base_part = jnp.dot(tokens, key_base_matrix, preferred_element_type=jnp.float32)
    base_half = lax.psum_scatter(base_part, "tp", scatter_dimension=1, tiled=True)
    delta_rows = returned.reshape(ad_count * capacity, up.shape[2])[position]
    return (base_half + delta_rows.astype(jnp.float32)).astype(jnp.bfloat16)


def solution(mesh):
    placed = (
        P(("grp", "ad"), "tp"),
        P(("grp", "ad"), None),
        P("tp", None),
        P(("grp", "ad"), "tp", None),
        P(("grp", "ad"), None, "tp"),
    )
    ad_count = mesh.shape["ad"]
    group = 4
    if ad_count in (group, 2 * group):
        on_device = functools.partial(by_features, ad_count, group)
    else:
        on_device = functools.partial(by_rows, ad_count)
    return jax.shard_map(
        on_device, mesh=mesh, in_specs=placed, out_specs=P(("grp", "ad"), "tp"), check_vma=False
    )
```

```python
import functools

import jax
import jax.numpy as jnp
from jax import lax
from jax.experimental import pallas as pl
from jax.experimental.pallas import tpu as pltpu
from jax.sharding import PartitionSpec as P

MESH = pl.DeviceIdType.MESH
LANES = 128
BASE_CHUNKS = 8
FACTORS = 4


def flip(index, bits):
    result, bit = index, 1
    while bit <= bits:
        if bits & bit:
            result = result + bit * (1 - 2 * lax.rem(lax.div(index, bit), 2))
        bit *= 2
    return result


def feature_kernel(
    ad_count, group,
    tok, idx, base, down, up, out,
    tok_own, base_all, gtok, gdown, gup, gidx,
    ids, acc, part_out, part_in, base_acc, base_in,
    local_sem, chunk_sem, tok_send, tok_recv, down_send, down_recv, up_send, up_recv,
    idx_ssem, idx_rsem, part_send, part_recv, base_send, base_recv,
):
    grp, me, tp = lax.axis_index("grp"), lax.axis_index("ad"), lax.axis_index("tp")
    rows, half_width = tok.shape
    slice_width = half_width // group
    rank, out_width = up.shape[1], up.shape[2]
    other = 1 - tp
    own_member = lax.rem(me, group)

    def device(slot, cross=0):
        return (grp, flip(me, slot), other if cross else tp)

    def columns(member):
        return pl.ds(pl.multiple_of(member * slice_width, slice_width), slice_width)

    loads = [
        pltpu.make_async_copy(
            down.at[0, :, columns(own_member)], gdown.at[pl.ds(0, rank)], local_sem.at[0]
        ),
        pltpu.make_async_copy(idx, gidx.at[0], local_sem.at[1]),
        pltpu.make_async_copy(tok, tok_own, local_sem.at[2]),
        pltpu.make_async_copy(tok.at[:, columns(own_member)], gtok.at[0], local_sem.at[3]),
        pltpu.make_async_copy(up.at[0], gup.at[pl.ds(0, rank)], local_sem.at[4]),
    ]
    for load in loads:
        load.start()
    depth = half_width // BASE_CHUNKS
    chunks = [
        pltpu.make_async_copy(
            base.at[pl.ds(c * depth, depth)], base_all.at[pl.ds(c * depth, depth)], chunk_sem.at[c]
        )
        for c in range(BASE_CHUNKS)
    ]
    for chunk in chunks:
        chunk.start()

    barrier = pltpu.get_barrier_semaphore()
    greeted = [(s, 0) for s in range(1, ad_count)] + [(s, 1) for s in range(group)]
    for s, cross in greeted:
        pl.semaphore_signal(barrier, inc=1, device_id=device(s, cross), device_id_type=MESH)
    pl.semaphore_wait(barrier, len(greeted))

    tok_copies = {}
    for s in range(group - 1, 0, -1):
        tok_copies[s] = pltpu.make_async_remote_copy(
            src_ref=tok.at[:, columns(lax.rem(flip(me, s), group))],
            dst_ref=gtok.at[s],
            send_sem=tok_send.at[s], recv_sem=tok_recv.at[s],
            device_id=device(s), device_id_type=MESH,
        )
        tok_copies[s].start()

    down_copies = {}
    for s in range(ad_count - 1, 0, -1):
        down_copies[s] = pltpu.make_async_remote_copy(
            src_ref=down.at[0, :, columns(lax.rem(flip(me, s), group))],
            dst_ref=gdown.at[pl.ds(s * rank, rank)],
            send_sem=down_send.at[s], recv_sem=down_recv.at[s],
            device_id=device(s), device_id_type=MESH,
        )
        down_copies[s].start()

    idx_copies = {}
    for s in range(group - 1, 0, -1):
        idx_copies[s] = pltpu.make_async_remote_copy(
            src_ref=idx, dst_ref=gidx.at[s],
            send_sem=idx_ssem.at[s], recv_sem=idx_rsem.at[s],
            device_id=device(s), device_id_type=MESH,
        )
        idx_copies[s].start()

    up_copies = {}

    def send_up(source, slot, to):
        up_copies[slot] = pltpu.make_async_remote_copy(
            src_ref=source, dst_ref=gup.at[pl.ds(slot * rank, rank)],
            send_sem=up_send.at[slot], recv_sem=up_recv.at[slot],
            device_id=device(to), device_id_type=MESH,
        )
        up_copies[slot].start()

    for s in list(range(ad_count - 2, 0, -2)) + [1]:
        send_up(up.at[0], s, s)

    loads[2].wait()
    base_acc[...] = jnp.zeros_like(base_acc)
    for chunk in chunks:
        chunk.wait()

    @pl.loop(0, BASE_CHUNKS)
    def _(c):
        span = pl.ds(pl.multiple_of(c * depth, depth), depth)
        base_acc[...] += jnp.dot(
            tok_own[:, span], base_all[span, :], preferred_element_type=jnp.float32
        )

    base_copy = pltpu.make_async_remote_copy(
        src_ref=base_acc.at[:, pl.ds(pl.multiple_of(other * out_width, out_width), out_width)],
        dst_ref=base_in,
        send_sem=base_send.at[0], recv_sem=base_recv.at[0],
        device_id=device(0, 1), device_id_type=MESH,
    )
    base_copy.start()

    for s in range(2, ad_count, 2):
        up_copies[s].wait_recv()
        send_up(gup.at[pl.ds(s * rank, rank)], s + 1, 1)

    loads[1].wait()
    for s in range(group):
        if s:
            idx_copies[s].wait_recv()
        ids[s] = jnp.broadcast_to(gidx[s], (LANES, rows)).astype(jnp.float32).T.astype(jnp.int32)
    loads[0].wait()
    loads[3].wait()
    for s in range(1, group):
        tok_copies[s].wait_recv()

    low = lax.broadcasted_iota(jnp.int32, (rows, LANES), 1) < rank
    for p in range(0, ad_count, FACTORS):
        for s in range(p, p + FACTORS):
            if s:
                down_copies[s].wait_recv()
        factors = gdown[p * rank:(p + FACTORS) * rank, :]
        for m in range(group):
            product = lax.dot_general(
                gtok[m], factors, (((1,), (1,)), ((), ())), preferred_element_type=jnp.float32
            )
            total = jnp.zeros((rows, LANES), jnp.float32) if p == 0 else acc[m]
            for k in range(0, FACTORS, 2):
                named = jnp.where(low, flip(me, p + k), flip(me, p + k + 1))
                total = jnp.where(ids[m] == named, product[:, k * rank:(k + 2) * rank], total)
            acc[m] = total

    part_copies = []
    for m in list(range(group - 1, 0, -1)) + [0]:
        whole = acc[m]
        whole = whole + pltpu.roll(whole, rank, 1)
        part_out[m] = jnp.where(low[:rows // 2], whole[:rows // 2], whole[rows // 2:])
        for cross in (0, 1):
            if m or cross:
                copy = pltpu.make_async_remote_copy(
                    src_ref=part_out.at[m], dst_ref=part_in.at[2 * m + cross],
                    send_sem=part_send.at[2 * m + cross], recv_sem=part_recv.at[2 * m + cross],
                    device_id=device(m, cross), device_id_type=MESH,
                )
                copy.start()
                part_copies.append(copy)

    base_copy.wait_recv()
    kept = base_acc[:, pl.ds(pl.multiple_of(tp * out_width, out_width), out_width)] + base_in[...]
    for s in range(1, ad_count, 2):
        up_copies[s].wait_recv()
    loads[4].wait()

    shrunk = part_out[0]
    for copy in part_copies:
        copy.wait_recv()
    for slot in range(1, 2 * group):
        shrunk = shrunk + part_in[slot]
    turned = pltpu.roll(shrunk, rank, 1)
    low_half = low[:rows // 2]
    spread = jnp.concatenate(
        [jnp.where(low_half, shrunk, turned), jnp.where(low_half, turned, shrunk)], axis=0
    )
    placed = []
    for p in range(0, ad_count, 2):
        named = jnp.where(low, flip(me, p), flip(me, p + 1))
        placed.append(jnp.where(ids[0] == named, spread, 0.0).astype(jnp.bfloat16))
    expanded = jnp.dot(
        jnp.concatenate(placed, axis=1), gup[...], preferred_element_type=jnp.float32
    ).astype(jnp.bfloat16)
    out[...] = (kept + expanded.astype(jnp.float32)).astype(jnp.bfloat16)

    for copies in (tok_copies, down_copies, idx_copies, up_copies):
        for s in copies:
            copies[s].wait_send()
    for copy in part_copies:
        copy.wait_send()
    base_copy.wait_send()


def by_features(ad_count, group, tokens, row_adapter_index, key_base_matrix, down, up):
    rows, half_width = tokens.shape
    key_width = key_base_matrix.shape[1]
    rank, out_width = up.shape[1], up.shape[2]
    slice_width = half_width // group
    bf16, f32, i32 = jnp.bfloat16, jnp.float32, jnp.int32
    dma = pltpu.SemaphoreType.DMA
    return pl.pallas_call(
        functools.partial(feature_kernel, ad_count, group),
        out_shape=jax.ShapeDtypeStruct((rows, out_width), bf16),
        in_specs=[pl.BlockSpec(memory_space=pl.ANY)] * 5,
        out_specs=pl.BlockSpec(memory_space=pltpu.VMEM),
        scratch_shapes=[
            pltpu.VMEM((rows, half_width), bf16),
            pltpu.VMEM((half_width, key_width), bf16),
            pltpu.VMEM((group, rows, slice_width), bf16),
            pltpu.VMEM((ad_count * rank, slice_width), bf16),
            pltpu.VMEM((ad_count * rank, out_width), bf16),
            pltpu.VMEM((group, 1, rows), i32),
            pltpu.VMEM((group, rows, LANES), i32),
            pltpu.VMEM((group, rows, LANES), f32),
            pltpu.VMEM((group, rows // 2, LANES), f32),
            pltpu.VMEM((2 * group, rows // 2, LANES), f32),
            pltpu.VMEM((rows, key_width), f32),
            pltpu.VMEM((rows, out_width), f32),
            dma((5,)), dma((BASE_CHUNKS,)),
            dma((group,)), dma((group,)),
            dma((ad_count,)), dma((ad_count,)),
            dma((ad_count,)), dma((ad_count,)),
            dma((group,)), dma((group,)),
            dma((2 * group,)), dma((2 * group,)),
            dma((1,)), dma((1,)),
        ],
        compiler_params=pltpu.CompilerParams(
            collective_id=0, has_side_effects=True, vmem_limit_bytes=63 * 1024 * 1024
        ),
        cost_estimate=pl.CostEstimate(
            flops=2 * rows * half_width * (key_width + 2 * ad_count * rank),
            bytes_accessed=2 * half_width * (key_width + 2 * rows + rank),
            transcendentals=0,
        ),
    )(tokens, row_adapter_index.reshape(1, rows), key_base_matrix, jnp.swapaxes(down, 1, 2), up)


def by_rows(ad_count, tokens, row_adapter_index, key_base_matrix, down, up):
    row_count, feature_half = tokens.shape
    capacity = max(2, 2 * row_count // ad_count)
    row_adapter = row_adapter_index[:, 0]
    one_hot = (row_adapter[:, None] == jnp.arange(ad_count, dtype=jnp.int32)[None, :]).astype(
        jnp.int32
    )
    earlier = jnp.cumsum(one_hot, axis=0) - one_hot
    position = row_adapter * capacity + jnp.sum(earlier * one_hot, axis=1)
    outgoing = jnp.zeros((ad_count * capacity, feature_half), jnp.bfloat16).at[position].set(tokens)
    outgoing = outgoing.reshape(ad_count, capacity, feature_half)
    received = lax.all_to_all(outgoing, "ad", split_axis=0, concat_axis=0, tiled=True)
    flat_rows = received.reshape(ad_count * capacity, feature_half)
    shrunk_part = jnp.dot(flat_rows, down[0], preferred_element_type=jnp.float32)
    shrunk = lax.psum(shrunk_part, "tp").astype(jnp.bfloat16)
    expanded = jnp.dot(shrunk, up[0], preferred_element_type=jnp.float32).astype(jnp.bfloat16)
    expanded = expanded.reshape(ad_count, capacity, up.shape[2])
    returned = lax.all_to_all(expanded, "ad", split_axis=0, concat_axis=0, tiled=True)
    base_part = jnp.dot(tokens, key_base_matrix, preferred_element_type=jnp.float32)
    base_half = lax.psum_scatter(base_part, "tp", scatter_dimension=1, tiled=True)
    delta_rows = returned.reshape(ad_count * capacity, up.shape[2])[position]
    return (base_half + delta_rows.astype(jnp.float32)).astype(jnp.bfloat16)


def solution(mesh):
    placed = (
        P(("grp", "ad"), "tp"),
        P(("grp", "ad"), None),
        P("tp", None),
        P(("grp", "ad"), "tp", None),
        P(("grp", "ad"), None, "tp"),
    )
    ad_count = mesh.shape["ad"]
    group = 4
    if ad_count in (group, 2 * group):
        on_device = functools.partial(by_features, ad_count, group)
    else:
        on_device = functools.partial(by_rows, ad_count)
    return jax.shard_map(
        on_device, mesh=mesh, in_specs=placed, out_specs=P(("grp", "ad"), "tp"), check_vma=False
    )
```

```python
import functools

import jax
import jax.numpy as jnp
from jax import lax
from jax.experimental import pallas as pl
from jax.experimental.pallas import tpu as pltpu
from jax.sharding import PartitionSpec as P

MESH = pl.DeviceIdType.MESH
LANES = 128
BASE_CHUNKS = 8
FACTORS = 2


def flip(index, bits):
    result, bit = index, 1
    while bit <= bits:
        if bits & bit:
            result = result + bit * (1 - 2 * lax.rem(lax.div(index, bit), 2))
        bit *= 2
    return result


def feature_kernel(
    ad_count, group,
    tok, idx, base, down, up, out,
    tok_own, base_all, gtok, gdown, gup, gidx,
    ids, acc, part_out, part_in, base_acc, base_in,
    local_sem, chunk_sem, tok_send, tok_recv, down_send, down_recv, up_send, up_recv,
    idx_ssem, idx_rsem, part_send, part_recv, base_send, base_recv,
):
    grp, me, tp = lax.axis_index("grp"), lax.axis_index("ad"), lax.axis_index("tp")
    rows, half_width = tok.shape
    slice_width = half_width // group
    rank, out_width = up.shape[1], up.shape[2]
    other = 1 - tp
    own_member = lax.rem(me, group)

    def device(slot, cross=0):
        return (grp, flip(me, slot), other if cross else tp)

    def columns(member):
        return pl.ds(pl.multiple_of(member * slice_width, slice_width), slice_width)

    loads = [
        pltpu.make_async_copy(
            down.at[0, :, columns(own_member)], gdown.at[pl.ds(0, rank)], local_sem.at[0]
        ),
        pltpu.make_async_copy(idx, gidx.at[0], local_sem.at[1]),
        pltpu.make_async_copy(tok, tok_own, local_sem.at[2]),
        pltpu.make_async_copy(tok.at[:, columns(own_member)], gtok.at[0], local_sem.at[3]),
        pltpu.make_async_copy(up.at[0], gup.at[pl.ds(0, rank)], local_sem.at[4]),
    ]
    for load in loads:
        load.start()
    depth = half_width // BASE_CHUNKS
    chunks = [
        pltpu.make_async_copy(
            base.at[pl.ds(c * depth, depth)], base_all.at[pl.ds(c * depth, depth)], chunk_sem.at[c]
        )
        for c in range(BASE_CHUNKS)
    ]
    for chunk in chunks:
        chunk.start()

    barrier = pltpu.get_barrier_semaphore()
    greeted = [(s, 0) for s in range(1, ad_count)] + [(s, 1) for s in range(group)]
    for s, cross in greeted:
        pl.semaphore_signal(barrier, inc=1, device_id=device(s, cross), device_id_type=MESH)
    pl.semaphore_wait(barrier, len(greeted))

    tok_copies = {}
    for s in range(group - 1, 0, -1):
        tok_copies[s] = pltpu.make_async_remote_copy(
            src_ref=tok.at[:, columns(lax.rem(flip(me, s), group))],
            dst_ref=gtok.at[s],
            send_sem=tok_send.at[s], recv_sem=tok_recv.at[s],
            device_id=device(s), device_id_type=MESH,
        )

    down_copies = {}
    for s in range(ad_count - 1, 0, -1):
        down_copies[s] = pltpu.make_async_remote_copy(
            src_ref=down.at[0, :, columns(lax.rem(flip(me, s), group))],
            dst_ref=gdown.at[pl.ds(s * rank, rank)],
            send_sem=down_send.at[s], recv_sem=down_recv.at[s],
            device_id=device(s), device_id_type=MESH,
        )

    idx_copies = {}
    for s in range(group - 1, 0, -1):
        idx_copies[s] = pltpu.make_async_remote_copy(
            src_ref=idx, dst_ref=gidx.at[s],
            send_sem=idx_ssem.at[s], recv_sem=idx_rsem.at[s],
            device_id=device(s), device_id_type=MESH,
        )

    up_copies = {}

    def send_up(source, slot, to):
        up_copies[slot] = pltpu.make_async_remote_copy(
            src_ref=source, dst_ref=gup.at[pl.ds(slot * rank, rank)],
            send_sem=up_send.at[slot], recv_sem=up_recv.at[slot],
            device_id=device(to), device_id_type=MESH,
        )

    direct = [1] + list(range(2, ad_count, 2))
    for s in direct:
        send_up(up.at[0], s, s)

    near, far = list(range(1, group)), list(range(group, ad_count))
    for s in near:
        idx_copies[s].start()
    for s in direct:
        up_copies[s].start()
    for s in sorted(far, key=lambda s: (s % 2, s)):
        down_copies[s].start()
    for s in near:
        tok_copies[s].start()
    for s in near:
        down_copies[s].start()

    loads[2].wait()
    base_acc[...] = jnp.zeros_like(base_acc)
    for chunk in chunks:
        chunk.wait()

    @pl.loop(0, BASE_CHUNKS)
    def _(c):
        span = pl.ds(pl.multiple_of(c * depth, depth), depth)
        base_acc[...] += jnp.dot(
            tok_own[:, span], base_all[span, :], preferred_element_type=jnp.float32
        )

    base_copy = pltpu.make_async_remote_copy(
        src_ref=base_acc.at[:, pl.ds(pl.multiple_of(other * out_width, out_width), out_width)],
        dst_ref=base_in,
        send_sem=base_send.at[0], recv_sem=base_recv.at[0],
        device_id=device(0, 1), device_id_type=MESH,
    )
    base_copy.start()

    for s in range(2, ad_count, 2):
        up_copies[s].wait_recv()
        send_up(gup.at[pl.ds(s * rank, rank)], s + 1, 1)
        up_copies[s + 1].start()

    loads[1].wait()
    for s in range(group):
        if s:
            idx_copies[s].wait_recv()
        ids[s] = jnp.broadcast_to(gidx[s], (LANES, rows)).astype(jnp.float32).T.astype(jnp.int32)
    loads[0].wait()
    loads[3].wait()
    for s in range(1, group):
        tok_copies[s].wait_recv()

    low = lax.broadcasted_iota(jnp.int32, (rows, LANES), 1) < rank
    for p in range(0, ad_count, FACTORS):
        for s in range(p, p + FACTORS):
            if s:
                down_copies[s].wait_recv()
        factors = gdown[p * rank:(p + FACTORS) * rank, :]
        for m in range(group):
            product = lax.dot_general(
                gtok[m], factors, (((1,), (1,)), ((), ())), preferred_element_type=jnp.float32
            )
            total = jnp.zeros((rows, LANES), jnp.float32) if p == 0 else acc[m]
            for k in range(0, FACTORS, 2):
                named = jnp.where(low, flip(me, p + k), flip(me, p + k + 1))
                total = jnp.where(ids[m] == named, product[:, k * rank:(k + 2) * rank], total)
            acc[m] = total

    part_copies = []
    for m in list(range(group - 1, 0, -1)) + [0]:
        whole = acc[m]
        whole = whole + pltpu.roll(whole, rank, 1)
        part_out[m] = jnp.where(low[:rows // 2], whole[:rows // 2], whole[rows // 2:])
        for cross in (0, 1):
            if m or cross:
                copy = pltpu.make_async_remote_copy(
                    src_ref=part_out.at[m], dst_ref=part_in.at[2 * m + cross],
                    send_sem=part_send.at[2 * m + cross], recv_sem=part_recv.at[2 * m + cross],
                    device_id=device(m, cross), device_id_type=MESH,
                )
                copy.start()
                part_copies.append(copy)

    base_copy.wait_recv()
    kept = base_acc[:, pl.ds(pl.multiple_of(tp * out_width, out_width), out_width)] + base_in[...]
    for s in range(1, ad_count, 2):
        up_copies[s].wait_recv()
    loads[4].wait()

    shrunk = part_out[0]
    for copy in part_copies:
        copy.wait_recv()
    for slot in range(1, 2 * group):
        shrunk = shrunk + part_in[slot]
    turned = pltpu.roll(shrunk, rank, 1)
    low_half = low[:rows // 2]
    spread = jnp.concatenate(
        [jnp.where(low_half, shrunk, turned), jnp.where(low_half, turned, shrunk)], axis=0
    )
    placed = []
    for p in range(0, ad_count, 2):
        named = jnp.where(low, flip(me, p), flip(me, p + 1))
        placed.append(jnp.where(ids[0] == named, spread, 0.0).astype(jnp.bfloat16))
    expanded = jnp.dot(
        jnp.concatenate(placed, axis=1), gup[...], preferred_element_type=jnp.float32
    ).astype(jnp.bfloat16)
    out[...] = (kept + expanded.astype(jnp.float32)).astype(jnp.bfloat16)

    for copies in (tok_copies, down_copies, idx_copies, up_copies):
        for s in copies:
            copies[s].wait_send()
    for copy in part_copies:
        copy.wait_send()
    base_copy.wait_send()


def by_features(ad_count, group, tokens, row_adapter_index, key_base_matrix, down, up):
    rows, half_width = tokens.shape
    key_width = key_base_matrix.shape[1]
    rank, out_width = up.shape[1], up.shape[2]
    slice_width = half_width // group
    bf16, f32, i32 = jnp.bfloat16, jnp.float32, jnp.int32
    dma = pltpu.SemaphoreType.DMA
    return pl.pallas_call(
        functools.partial(feature_kernel, ad_count, group),
        out_shape=jax.ShapeDtypeStruct((rows, out_width), bf16),
        in_specs=[pl.BlockSpec(memory_space=pl.ANY)] * 5,
        out_specs=pl.BlockSpec(memory_space=pltpu.VMEM),
        scratch_shapes=[
            pltpu.VMEM((rows, half_width), bf16),
            pltpu.VMEM((half_width, key_width), bf16),
            pltpu.VMEM((group, rows, slice_width), bf16),
            pltpu.VMEM((ad_count * rank, slice_width), bf16),
            pltpu.VMEM((ad_count * rank, out_width), bf16),
            pltpu.VMEM((group, 1, rows), i32),
            pltpu.VMEM((group, rows, LANES), i32),
            pltpu.VMEM((group, rows, LANES), f32),
            pltpu.VMEM((group, rows // 2, LANES), f32),
            pltpu.VMEM((2 * group, rows // 2, LANES), f32),
            pltpu.VMEM((rows, key_width), f32),
            pltpu.VMEM((rows, out_width), f32),
            dma((5,)), dma((BASE_CHUNKS,)),
            dma((group,)), dma((group,)),
            dma((ad_count,)), dma((ad_count,)),
            dma((ad_count,)), dma((ad_count,)),
            dma((group,)), dma((group,)),
            dma((2 * group,)), dma((2 * group,)),
            dma((1,)), dma((1,)),
        ],
        compiler_params=pltpu.CompilerParams(
            collective_id=0, has_side_effects=True, vmem_limit_bytes=63 * 1024 * 1024
        ),
        cost_estimate=pl.CostEstimate(
            flops=2 * rows * half_width * (key_width + 2 * ad_count * rank),
            bytes_accessed=2 * half_width * (key_width + 2 * rows + rank),
            transcendentals=0,
        ),
    )(tokens, row_adapter_index.reshape(1, rows), key_base_matrix, jnp.swapaxes(down, 1, 2), up)


def by_rows(ad_count, tokens, row_adapter_index, key_base_matrix, down, up):
    row_count, feature_half = tokens.shape
    capacity = max(2, 2 * row_count // ad_count)
    row_adapter = row_adapter_index[:, 0]
    one_hot = (row_adapter[:, None] == jnp.arange(ad_count, dtype=jnp.int32)[None, :]).astype(
        jnp.int32
    )
    earlier = jnp.cumsum(one_hot, axis=0) - one_hot
    position = row_adapter * capacity + jnp.sum(earlier * one_hot, axis=1)
    outgoing = jnp.zeros((ad_count * capacity, feature_half), jnp.bfloat16).at[position].set(tokens)
    outgoing = outgoing.reshape(ad_count, capacity, feature_half)
    received = lax.all_to_all(outgoing, "ad", split_axis=0, concat_axis=0, tiled=True)
    flat_rows = received.reshape(ad_count * capacity, feature_half)
    shrunk_part = jnp.dot(flat_rows, down[0], preferred_element_type=jnp.float32)
    shrunk = lax.psum(shrunk_part, "tp").astype(jnp.bfloat16)
    expanded = jnp.dot(shrunk, up[0], preferred_element_type=jnp.float32).astype(jnp.bfloat16)
    expanded = expanded.reshape(ad_count, capacity, up.shape[2])
    returned = lax.all_to_all(expanded, "ad", split_axis=0, concat_axis=0, tiled=True)
    base_part = jnp.dot(tokens, key_base_matrix, preferred_element_type=jnp.float32)
    base_half = lax.psum_scatter(base_part, "tp", scatter_dimension=1, tiled=True)
    delta_rows = returned.reshape(ad_count * capacity, up.shape[2])[position]
    return (base_half + delta_rows.astype(jnp.float32)).astype(jnp.bfloat16)


def solution(mesh):
    placed = (
        P(("grp", "ad"), "tp"),
        P(("grp", "ad"), None),
        P("tp", None),
        P(("grp", "ad"), "tp", None),
        P(("grp", "ad"), None, "tp"),
    )
    ad_count = mesh.shape["ad"]
    group = 4
    if ad_count in (group, 2 * group):
        on_device = functools.partial(by_features, ad_count, group)
    else:
        on_device = functools.partial(by_rows, ad_count)
    return jax.shard_map(
        on_device, mesh=mesh, in_specs=placed, out_specs=P(("grp", "ad"), "tp"), check_vma=False
    )
```

```python
import functools

import jax
import jax.numpy as jnp
from jax import lax
from jax.experimental import pallas as pl
from jax.experimental.pallas import tpu as pltpu
from jax.sharding import PartitionSpec as P

MESH = pl.DeviceIdType.MESH
LANES = 128
BASE_CHUNKS = 8
FACTORS = 2


def flip(index, bits):
    result, bit = index, 1
    while bit <= bits:
        if bits & bit:
            result = result + bit * (1 - 2 * lax.rem(lax.div(index, bit), 2))
        bit *= 2
    return result


def feature_kernel(
    ad_count, group,
    tok, idx, base, down, up, out,
    tok_own, base_all, gtok, gdown, gup, gidx,
    ids, acc, part_out, part_in, base_acc, base_in,
    local_sem, chunk_sem, tok_send, tok_recv, down_send, down_recv, up_send, up_recv,
    idx_ssem, idx_rsem, part_send, part_recv, base_send, base_recv,
):
    grp, me, tp = lax.axis_index("grp"), lax.axis_index("ad"), lax.axis_index("tp")
    rows, half_width = tok.shape
    slice_width = half_width // group
    rank, out_width = up.shape[1], up.shape[2]
    other = 1 - tp
    own_member = lax.rem(me, group)

    def device(slot, cross=0):
        return (grp, flip(me, slot), other if cross else tp)

    def columns(member):
        return pl.ds(pl.multiple_of(member * slice_width, slice_width), slice_width)

    barrier = pltpu.get_barrier_semaphore()
    greeted = [(s, 0) for s in range(1, ad_count)] + [(s, 1) for s in range(group)]
    for s, cross in greeted:
        pl.semaphore_signal(barrier, inc=1, device_id=device(s, cross), device_id_type=MESH)

    loads = [
        pltpu.make_async_copy(
            down.at[0, :, columns(own_member)], gdown.at[pl.ds(0, rank)], local_sem.at[0]
        ),
        pltpu.make_async_copy(idx, gidx.at[0], local_sem.at[1]),
        pltpu.make_async_copy(tok, tok_own, local_sem.at[2]),
        pltpu.make_async_copy(tok.at[:, columns(own_member)], gtok.at[0], local_sem.at[3]),
        pltpu.make_async_copy(up.at[0], gup.at[pl.ds(0, rank)], local_sem.at[4]),
    ]
    for load in loads:
        load.start()
    depth = half_width // BASE_CHUNKS
    chunks = [
        pltpu.make_async_copy(
            base.at[pl.ds(c * depth, depth)], base_all.at[pl.ds(c * depth, depth)], chunk_sem.at[c]
        )
        for c in range(BASE_CHUNKS)
    ]

    pl.semaphore_wait(barrier, len(greeted))

    tok_copies = {}
    for s in range(group - 1, 0, -1):
        tok_copies[s] = pltpu.make_async_remote_copy(
            src_ref=tok.at[:, columns(lax.rem(flip(me, s), group))],
            dst_ref=gtok.at[s],
            send_sem=tok_send.at[s], recv_sem=tok_recv.at[s],
            device_id=device(s), device_id_type=MESH,
        )

    down_copies = {}
    for s in range(ad_count - 1, 0, -1):
        down_copies[s] = pltpu.make_async_remote_copy(
            src_ref=down.at[0, :, columns(lax.rem(flip(me, s), group))],
            dst_ref=gdown.at[pl.ds(s * rank, rank)],
            send_sem=down_send.at[s], recv_sem=down_recv.at[s],
            device_id=device(s), device_id_type=MESH,
        )

    idx_copies = {}
    for s in range(group - 1, 0, -1):
        idx_copies[s] = pltpu.make_async_remote_copy(
            src_ref=idx, dst_ref=gidx.at[s],
            send_sem=idx_ssem.at[s], recv_sem=idx_rsem.at[s],
            device_id=device(s), device_id_type=MESH,
        )

    up_copies = {}

    def send_up(source, slot, to):
        up_copies[slot] = pltpu.make_async_remote_copy(
            src_ref=source, dst_ref=gup.at[pl.ds(slot * rank, rank)],
            send_sem=up_send.at[slot], recv_sem=up_recv.at[slot],
            device_id=device(to), device_id_type=MESH,
        )

    direct = [1] + list(range(2, ad_count, 2))
    for s in direct:
        send_up(up.at[0], s, s)

    near, far = list(range(1, group)), list(range(group, ad_count))
    for s in near:
        idx_copies[s].start()
    for s in direct:
        up_copies[s].start()
    for s in sorted(far, key=lambda s: (s % 2, s)):
        down_copies[s].start()
    for s in near:
        tok_copies[s].start()
    for s in near:
        down_copies[s].start()

    for chunk in chunks:
        chunk.start()
    loads[2].wait()
    base_acc[...] = jnp.zeros_like(base_acc)
    for chunk in chunks:
        chunk.wait()

    @pl.loop(0, BASE_CHUNKS)
    def _(c):
        span = pl.ds(pl.multiple_of(c * depth, depth), depth)
        base_acc[...] += jnp.dot(
            tok_own[:, span], base_all[span, :], preferred_element_type=jnp.float32
        )

    base_copy = pltpu.make_async_remote_copy(
        src_ref=base_acc.at[:, pl.ds(pl.multiple_of(other * out_width, out_width), out_width)],
        dst_ref=base_in,
        send_sem=base_send.at[0], recv_sem=base_recv.at[0],
        device_id=device(0, 1), device_id_type=MESH,
    )
    base_copy.start()

    for s in range(2, ad_count, 2):
        up_copies[s].wait_recv()
        send_up(gup.at[pl.ds(s * rank, rank)], s + 1, 1)
        up_copies[s + 1].start()

    loads[1].wait()
    for s in range(group):
        if s:
            idx_copies[s].wait_recv()
        ids[s] = jnp.broadcast_to(gidx[s], (LANES, rows)).astype(jnp.float32).T.astype(jnp.int32)
    loads[0].wait()
    loads[3].wait()
    for s in range(1, group):
        tok_copies[s].wait_recv()

    low = lax.broadcasted_iota(jnp.int32, (rows, LANES), 1) < rank
    for p in range(0, ad_count, FACTORS):
        for s in range(p, p + FACTORS):
            if s:
                down_copies[s].wait_recv()
        factors = gdown[p * rank:(p + FACTORS) * rank, :]
        for m in range(group):
            product = lax.dot_general(
                gtok[m], factors, (((1,), (1,)), ((), ())), preferred_element_type=jnp.float32
            )
            total = jnp.zeros((rows, LANES), jnp.float32) if p == 0 else acc[m]
            for k in range(0, FACTORS, 2):
                named = jnp.where(low, flip(me, p + k), flip(me, p + k + 1))
                total = jnp.where(ids[m] == named, product[:, k * rank:(k + 2) * rank], total)
            acc[m] = total

    part_copies = []
    for m in list(range(group - 1, 0, -1)) + [0]:
        whole = acc[m]
        whole = whole + pltpu.roll(whole, rank, 1)
        part_out[m] = jnp.where(low[:rows // 2], whole[:rows // 2], whole[rows // 2:])
        for cross in (0, 1):
            if m or cross:
                copy = pltpu.make_async_remote_copy(
                    src_ref=part_out.at[m], dst_ref=part_in.at[2 * m + cross],
                    send_sem=part_send.at[2 * m + cross], recv_sem=part_recv.at[2 * m + cross],
                    device_id=device(m, cross), device_id_type=MESH,
                )
                copy.start()
                part_copies.append(copy)

    base_copy.wait_recv()
    kept = base_acc[:, pl.ds(pl.multiple_of(tp * out_width, out_width), out_width)] + base_in[...]
    for s in range(1, ad_count, 2):
        up_copies[s].wait_recv()
    loads[4].wait()

    shrunk = part_out[0]
    for copy in part_copies:
        copy.wait_recv()
    for slot in range(1, 2 * group):
        shrunk = shrunk + part_in[slot]
    turned = pltpu.roll(shrunk, rank, 1)
    low_half = low[:rows // 2]
    spread = jnp.concatenate(
        [jnp.where(low_half, shrunk, turned), jnp.where(low_half, turned, shrunk)], axis=0
    )
    placed = []
    for p in range(0, ad_count, 2):
        named = jnp.where(low, flip(me, p), flip(me, p + 1))
        placed.append(jnp.where(ids[0] == named, spread, 0.0).astype(jnp.bfloat16))
    expanded = jnp.dot(
        jnp.concatenate(placed, axis=1), gup[...], preferred_element_type=jnp.float32
    ).astype(jnp.bfloat16)
    out[...] = (kept + expanded.astype(jnp.float32)).astype(jnp.bfloat16)

    for copies in (tok_copies, down_copies, idx_copies, up_copies):
        for s in copies:
            copies[s].wait_send()
    for copy in part_copies:
        copy.wait_send()
    base_copy.wait_send()


def by_features(ad_count, group, tokens, row_adapter_index, key_base_matrix, down, up):
    rows, half_width = tokens.shape
    key_width = key_base_matrix.shape[1]
    rank, out_width = up.shape[1], up.shape[2]
    slice_width = half_width // group
    bf16, f32, i32 = jnp.bfloat16, jnp.float32, jnp.int32
    dma = pltpu.SemaphoreType.DMA
    return pl.pallas_call(
        functools.partial(feature_kernel, ad_count, group),
        out_shape=jax.ShapeDtypeStruct((rows, out_width), bf16),
        in_specs=[pl.BlockSpec(memory_space=pl.ANY)] * 5,
        out_specs=pl.BlockSpec(memory_space=pltpu.VMEM),
        scratch_shapes=[
            pltpu.VMEM((rows, half_width), bf16),
            pltpu.VMEM((half_width, key_width), bf16),
            pltpu.VMEM((group, rows, slice_width), bf16),
            pltpu.VMEM((ad_count * rank, slice_width), bf16),
            pltpu.VMEM((ad_count * rank, out_width), bf16),
            pltpu.VMEM((group, 1, rows), i32),
            pltpu.VMEM((group, rows, LANES), i32),
            pltpu.VMEM((group, rows, LANES), f32),
            pltpu.VMEM((group, rows // 2, LANES), f32),
            pltpu.VMEM((2 * group, rows // 2, LANES), f32),
            pltpu.VMEM((rows, key_width), f32),
            pltpu.VMEM((rows, out_width), f32),
            dma((5,)), dma((BASE_CHUNKS,)),
            dma((group,)), dma((group,)),
            dma((ad_count,)), dma((ad_count,)),
            dma((ad_count,)), dma((ad_count,)),
            dma((group,)), dma((group,)),
            dma((2 * group,)), dma((2 * group,)),
            dma((1,)), dma((1,)),
        ],
        compiler_params=pltpu.CompilerParams(
            collective_id=0, has_side_effects=True, vmem_limit_bytes=63 * 1024 * 1024
        ),
        cost_estimate=pl.CostEstimate(
            flops=2 * rows * half_width * (key_width + 2 * ad_count * rank),
            bytes_accessed=2 * half_width * (key_width + 2 * rows + rank),
            transcendentals=0,
        ),
    )(tokens, row_adapter_index.reshape(1, rows), key_base_matrix, jnp.swapaxes(down, 1, 2), up)


def by_rows(ad_count, tokens, row_adapter_index, key_base_matrix, down, up):
    row_count, feature_half = tokens.shape
    capacity = max(2, 2 * row_count // ad_count)
    row_adapter = row_adapter_index[:, 0]
    one_hot = (row_adapter[:, None] == jnp.arange(ad_count, dtype=jnp.int32)[None, :]).astype(
        jnp.int32
    )
    earlier = jnp.cumsum(one_hot, axis=0) - one_hot
    position = row_adapter * capacity + jnp.sum(earlier * one_hot, axis=1)
    outgoing = jnp.zeros((ad_count * capacity, feature_half), jnp.bfloat16).at[position].set(tokens)
    outgoing = outgoing.reshape(ad_count, capacity, feature_half)
    received = lax.all_to_all(outgoing, "ad", split_axis=0, concat_axis=0, tiled=True)
    flat_rows = received.reshape(ad_count * capacity, feature_half)
    shrunk_part = jnp.dot(flat_rows, down[0], preferred_element_type=jnp.float32)
    shrunk = lax.psum(shrunk_part, "tp").astype(jnp.bfloat16)
    expanded = jnp.dot(shrunk, up[0], preferred_element_type=jnp.float32).astype(jnp.bfloat16)
    expanded = expanded.reshape(ad_count, capacity, up.shape[2])
    returned = lax.all_to_all(expanded, "ad", split_axis=0, concat_axis=0, tiled=True)
    base_part = jnp.dot(tokens, key_base_matrix, preferred_element_type=jnp.float32)
    base_half = lax.psum_scatter(base_part, "tp", scatter_dimension=1, tiled=True)
    delta_rows = returned.reshape(ad_count * capacity, up.shape[2])[position]
    return (base_half + delta_rows.astype(jnp.float32)).astype(jnp.bfloat16)


def solution(mesh):
    placed = (
        P(("grp", "ad"), "tp"),
        P(("grp", "ad"), None),
        P("tp", None),
        P(("grp", "ad"), "tp", None),
        P(("grp", "ad"), None, "tp"),
    )
    ad_count = mesh.shape["ad"]
    group = 4
    if ad_count in (group, 2 * group):
        on_device = functools.partial(by_features, ad_count, group)
    else:
        on_device = functools.partial(by_rows, ad_count)
    return jax.shard_map(
        on_device, mesh=mesh, in_specs=placed, out_specs=P(("grp", "ad"), "tp"), check_vma=False
    )
```
